256 devices in a mesh: group: 8 (over z), store: 32 (over x, y, core).
Axes of the slice: x: 4, y: 4, z: 8, core: 2. Of those that a mesh axis runs over, the one named last changes fastest.
Arguments:
- features: bfloat16 [262144, 256], P(('group', 'store')), may hold values from -6 to 6
- past_hidden: bfloat16 [2, 262144, 256], P(None, ('group', 'store')), may hold values from 0 to 2
- past_grads: bfloat16 [2, 262144, 256], P(None, ('group', 'store')), may hold values from -6 to 6
- cotangent: bfloat16 [262144, 256], P(('group', 'store')), may hold values from -24 to 24
- weights: bfloat16 [3, 256, 256], replicated, may hold values from -0.375 to 0.375
- inner_tiles: bfloat16 [2048, 3, 128, 128], P(('group', 'store')), as said below
- inner_blocks: int32 [2048, 3], P(('group', 'store')), may hold values from 0 to 7, all different within a row
- outer_tiles: bfloat16 [2048, 3, 128, 128], P(('group', 'store')), as said below
- outer_blocks: int32 [2048, 3], P(('group', 'store')), may hold values from 0 to 7, all different within a row
- slot_rows: int32 [256, 1024], P(('group', 'store')), may hold values from 0 to 1023
- slot_counts: int32 [256, 32], P(('group', 'store')), may hold values from 1 to 32, as said below
Outputs:
- hidden_out: bfloat16 [3, 262144, 256], P(None, ('group', 'store'))
- grad_out: bfloat16 [2, 262144, 256], P(None, ('group', 'store'))
- weight_grad: float32 [3, 256, 256], replicated
The draws below stay inside these ranges and needn't reach their ends.
Inputs may be any that keep to these rules, and one draw needn't show every extreme that they name: `slot_counts`: live halo slots of a device for one owner; every device has all 32 slots live for some owner, and some device for every owner. `slot_rows`: row within the owner's cluster; slots past the owner's count are padding. `inner_blocks`: distinct within a block row. `outer_blocks`: distinct within a block row. `inner_tiles`: nonnegative edge weights, most of them zero. `outer_tiles`: nonnegative edge weights, most of them zero.
All inputs are finite; a program needn't handle non-finite values.
Results may differ from the reference program's by a relative error of at most 0.0052.
Values may be sent and summed in bfloat16 or wider, within the bound.
A program may use at most 64 MiB of HBM per device.

```python
import math
import jax
import jax.numpy as jnp
from jax import lax

D = 256
LAYERS = 3
TILE = 128
TILES_IN = 3
TILES_OUT = 3
CLUSTER = 1024
HALO = 1024
OWNERS = 32
CAP = 32
NODES = 262144
BLOCKS = 2048
DEVICES = 256


def edge_weights(key, out_shape, span_ratio):
    key_keep, key_size = jax.random.split(key)
    keep_mask = jax.random.uniform(key_keep, out_shape) < 8.0 / TILE
    top_weight = 0.44 / (TILES_IN + TILES_OUT)
    uniform_val = jax.random.uniform(key_size, out_shape)
    weight_val = top_weight * jnp.exp(-uniform_val * jnp.log(span_ratio))
    return jnp.where(keep_mask, weight_val, 0.0).astype(jnp.float32)


def draw_inner_tiles(key, part):
    key = jax.random.fold_in(key, 5)
    span_ratio = 30.0
    return edge_weights(key, (BLOCKS, TILES_IN, TILE, TILE), span_ratio).astype(jnp.bfloat16)


def draw_outer_tiles(key, part):
    key = jax.random.fold_in(key, 7)
    span_ratio = 30.0
    return edge_weights(key, (BLOCKS, TILES_OUT, TILE, TILE), span_ratio).astype(jnp.bfloat16)


def draw_slot_counts(key, part):
    key = jax.random.fold_in(key, 11)
    key_base, key_heat, key_pick, key_full = jax.random.split(key, 4)
    device_total = NODES // CLUSTER
    base_count = jax.random.randint(key_base, (device_total, OWNERS), 1, CAP + 1)
    heat_level = jax.random.randint(key_heat, (1, OWNERS), 0, 4)
    boosted = jnp.minimum(base_count * (1 + 2 * (heat_level == 0).astype(jnp.int32)), CAP)
    pick_owner = jax.random.randint(key_pick, (device_total, 1), 0, OWNERS)
    owner_index = jnp.arange(OWNERS, dtype=jnp.int32)[None, :]
    boosted = jnp.where(owner_index == pick_owner, CAP, boosted)
    full_device = jax.random.randint(key_full, (), 0, device_total)
    device_index = jnp.arange(device_total, dtype=jnp.int32)[:, None]
    boosted = jnp.where(device_index == full_device, CAP, boosted)
    return boosted.astype(jnp.int32)


def with_ends(array, rng, smallest, top_value):
    longest = array.shape.index(max(array.shape))
    spots = []
    for shift in (0, 1):
        where = [jax.random.randint(jax.random.fold_in(rng, axis), (), 0, length) for axis, length in enumerate(array.shape)]
        where[longest] = (where[longest] + shift) % array.shape[longest]
        spots.append(tuple(where))
    return array.at[spots[0]].set(smallest).at[spots[1]].set(top_value)


def raised(entries, own_key, source, target, shards_of, factor):
    def block_of(axis_at):
        return (jnp.arange(entries.shape[axis_at]) // (entries.shape[axis_at] // shards_of)).reshape((-1,) + (1,) * (entries.ndim - 1 - axis_at))

    near = jax.random.permutation(own_key, shards_of)[block_of(target)]
    other_side = (block_of(target) + shards_of // 2) % shards_of
    return jnp.where((block_of(source) == near) | (block_of(source) == other_side), factor * entries, entries)


def block_levels(key, dims, cuts, smallest, high):
    level, own = 1.0, jax.random.fold_in(key, 6)
    for dim, shards_of in cuts:
        heights = jnp.exp(jax.random.uniform(jax.random.fold_in(own, dim), (shards_of,), jnp.float32, smallest / len(cuts), high / len(cuts)))
        level = level * jnp.repeat(heights, dims[dim] // shards_of).reshape([-1 if axis == dim else 1 for axis in range(len(dims))])
    return level


def distinct(own_key, rows, number_of, top, lift):
    order = jax.random.permutation(jax.random.fold_in(own_key, 1), number_of)
    favour = order
    for power in range(3):
        favour = favour * favour // number_of
    favour = favour * lift // number_of
    chance = jax.random.randint(jax.random.fold_in(own_key, 2), (rows, number_of), 0, 4096) + favour
    holders = jax.random.permutation(jax.random.fold_in(own_key, 3), rows)[jnp.arange(number_of) % rows]
    chance = jnp.where(jnp.arange(rows)[:, None] == holders[None, :], 1 << 14, chance)
    merit = chance * number_of + jnp.arange(number_of)
    return lax.top_k(merit.astype(jnp.int32), top)[1].astype(jnp.int32)


def noise(stream_key, shape, scale, limit, shards=(), kind=jnp.bfloat16):
    drawn = jax.random.normal(stream_key, shape, jnp.float32) * scale
    if len(shards) > 0:
        drawn = block_levels(stream_key, shape, shards, -0.22, 0.18) * drawn
    return jnp.clip(drawn, min=-limit, max=limit).astype(kind)


def gaussian_with(key, dims, width, most, cuts, heavy, kind=jnp.bfloat16):
    values = width * jax.random.normal(key, dims, jnp.float32)
    if cuts:
        values = values * block_levels(key, dims, cuts, -0.22, 0.18)
    return jnp.clip(raised(values, jax.random.fold_in(key, 3), *heavy), -most, most).astype(kind)


def setup_inputs(seed: int = 0) -> dict:
    seeds = jax.random.split(jax.random.key(seed), 12)
    features = noise(seeds[0], (NODES, D), 1.0, 6.0, ((0, 256),))
    past_hidden = jnp.clip(2.0 * jax.random.uniform(seeds[1], (LAYERS - 1, NODES, D), jnp.float32) ** block_levels(seeds[1], (LAYERS - 1, NODES, D), ((1, 256),), -0.2, 0.2), 0.0, 2.0).astype(jnp.bfloat16)
    past_grads = noise(seeds[2], (LAYERS - 1, NODES, D), 1.0, 6.0, ((1, 256),))
    cotangent = gaussian_with(seeds[3], (NODES, D), 1.0, 24.0, ((0, 256),), (0, 1, 256, 6.0))
    weights = noise(seeds[4], (LAYERS, D, D), D ** -0.5, 0.375)
    inner_tiles = draw_inner_tiles(jax.random.fold_in(seeds[11], 71), 0)
    inner_blocks = distinct(seeds[6], BLOCKS, CLUSTER // TILE, TILES_IN, 0)
    outer_tiles = draw_outer_tiles(jax.random.fold_in(seeds[11], 71), 0)
    outer_blocks = distinct(seeds[8], BLOCKS, HALO // TILE, TILES_OUT, 0)
    slot_rows = with_ends(jax.random.randint(seeds[9], (DEVICES, HALO), 0, CLUSTER), jax.random.fold_in(seeds[9], 1), 0, CLUSTER - 1).astype(jnp.int32)
    slot_counts = draw_slot_counts(jax.random.fold_in(seeds[11], 71), 0)
    return {"features": features, "past_hidden": past_hidden, "past_grads": past_grads, "cotangent": cotangent, "weights": weights, "inner_tiles": inner_tiles, "inner_blocks": inner_blocks, "outer_tiles": outer_tiles, "outer_blocks": outer_blocks, "slot_rows": slot_rows, "slot_counts": slot_counts}


RESTART = 0.1

def beta_of(layer_idx):
    return math.log(0.5 / (layer_idx + 1) + 1.0)

def block_product(tile_set, block_ids, source):
    feat_dim = source.shape[-1]
    tile_len = tile_set.shape[-1]
    blocks = source.reshape(-1, tile_len, feat_dim)[block_ids]
    summed = jnp.einsum('bkij,bkjd->bid', tile_set.astype(jnp.float32), blocks.astype(jnp.float32))
    return summed.reshape(-1, feat_dim)

def transposed_product(tile_set, block_ids, source):
    feat_dim = source.shape[-1]
    tile_len = tile_set.shape[-1]
    block_count = tile_set.shape[0]
    shaped = source.reshape(block_count, tile_len, feat_dim).astype(jnp.float32)
    pieces = jnp.einsum('bkij,bid->bkjd', tile_set.astype(jnp.float32), shaped)
    summed = jnp.zeros((block_count, tile_len, feat_dim), jnp.float32)
    summed = summed.at[block_ids.reshape(-1)].add(pieces.reshape(-1, tile_len, feat_dim))
    return summed.reshape(-1, feat_dim)

def reference(features, past_hidden, past_grads, cotangent, weights, inner_tiles, inner_blocks, outer_tiles, outer_blocks, slot_rows, slot_counts):
    feat_dim = features.shape[1]
    device_total = features.shape[0] // CLUSTER
    layers = weights.shape[0]
    dev_blocks = CLUSTER // TILE
    slot_index = jnp.arange(HALO, dtype=jnp.int32)
    slot_owner = slot_index // CAP
    slot_place = slot_index % CAP

    def one_device(carry_sum, device_idx):
        row_start = device_idx * CLUSTER
        block_start = device_idx * dev_blocks
        group_base = device_idx // OWNERS * (OWNERS * CLUSTER)
        slot_nodes = group_base + slot_owner * CLUSTER + slot_rows[device_idx]
        live_mask = slot_place < slot_counts[device_idx][slot_owner]

        def pull_rows(source_table):
            return jnp.where(live_mask[:, None], source_table[slot_nodes], jnp.zeros((), source_table.dtype))

        def own_rows(source_table):
            return lax.dynamic_slice_in_dim(source_table, row_start, CLUSTER, 0)
        inner_set = lax.dynamic_slice_in_dim(inner_tiles, block_start, dev_blocks, 0)
        inner_ids = lax.dynamic_slice_in_dim(inner_blocks, block_start, dev_blocks, 0)
        outer_set = lax.dynamic_slice_in_dim(outer_tiles, block_start, dev_blocks, 0)
        outer_ids = lax.dynamic_slice_in_dim(outer_blocks, block_start, dev_blocks, 0)
        first_rows = own_rows(features)
        first_f32 = first_rows.astype(jnp.float32)
        hidden = first_rows
        mixed_list = []
        pre_list = []
        hidden_list = []
        for layer_idx in range(layers):
            beta_now = beta_of(layer_idx)
            outside = pull_rows(features if layer_idx == 0 else past_hidden[layer_idx - 1])
            aggregate = block_product(inner_set, inner_ids, hidden) + block_product(outer_set, outer_ids, outside)
            mixed_rows = ((1.0 - RESTART) * aggregate + RESTART * first_f32).astype(jnp.bfloat16)
            pre_act = (1.0 - beta_now) * mixed_rows.astype(jnp.float32) + beta_now * jnp.dot(mixed_rows, weights[layer_idx], preferred_element_type=jnp.float32)
            hidden = jax.nn.silu(pre_act).astype(jnp.bfloat16)
            mixed_list.append(mixed_rows)
            pre_list.append(pre_act)
            hidden_list.append(hidden)
        upstream = own_rows(cotangent).astype(jnp.float32)
        w_terms = [None] * layers
        agg_grads = [None] * (layers - 1)
        for layer_idx in reversed(range(layers)):
            beta_now = beta_of(layer_idx)
            pre_act = pre_list[layer_idx]
            sigmoid_val = jax.nn.sigmoid(pre_act)
            pre_grad = (upstream * sigmoid_val * (1.0 + pre_act * (1.0 - sigmoid_val))).astype(jnp.bfloat16)
            w_terms[layer_idx] = beta_now * jnp.dot(mixed_list[layer_idx].T, pre_grad, preferred_element_type=jnp.float32)
            if layer_idx >= 1:
                mix_grad = (1.0 - beta_now) * pre_grad.astype(jnp.float32) + beta_now * jnp.dot(pre_grad, weights[layer_idx].T, preferred_element_type=jnp.float32)
                agg_grad = ((1.0 - RESTART) * mix_grad).astype(jnp.bfloat16)
                agg_grads[layer_idx - 1] = agg_grad
                outside = pull_rows(past_grads[layer_idx - 1])
                upstream = transposed_product(inner_set, inner_ids, agg_grad) + block_product(outer_set, outer_ids, outside)
        return (carry_sum + jnp.stack(w_terms), (jnp.stack(hidden_list), jnp.stack(agg_grads)))
    start_sum = jnp.zeros((layers, feat_dim, feat_dim), jnp.float32)
    weight_total, stacked_out = lax.scan(one_device, start_sum, jnp.arange(device_total, dtype=jnp.int32))
    hidden_all, grad_all = stacked_out
    hidden_out = jnp.transpose(hidden_all, (1, 0, 2, 3)).reshape(layers, -1, feat_dim)
    grad_out = jnp.transpose(grad_all, (1, 0, 2, 3)).reshape(layers - 1, -1, feat_dim)
    weight_grad = weight_total * (1.0 / math.sqrt(NODES))
    return (hidden_out, grad_out, weight_grad)
```

```python
import functools
import math

import jax
import jax.numpy as jnp
from jax import lax
from jax.experimental import pallas as pl
from jax.experimental.pallas import tpu as pltpu
from jax.sharding import PartitionSpec as P

RESTART = 0.1
MESH = pl.DeviceIdType.MESH
BF = jnp.bfloat16
F32 = jnp.float32


def beta_of(layer_idx):
    return math.log(0.5 / (layer_idx + 1) + 1.0)


def dot(lhs, rhs):
    return jnp.dot(lhs, rhs, preferred_element_type=F32)


def dot_nt(lhs, rhs):
    return lax.dot_general(lhs, rhs, (((1,), (1,)), ((), ())), preferred_element_type=F32)


def step_kernel(
    groups, owners, node_total,
    feat_hbm, past_h_hbm, past_g_hbm, cot_hbm, w_hbm, itile_hbm, iblk_hbm, otile_hbm, oblk_hbm,
    rows_hbm, cnt_hbm,
    hid_hbm, gout_hbm, wg_hbm,
    table, cot, wts, itile, otile, iblk, oblk, cnt,
    idx, onehot, sendbuf, recv, a_in, a_out, a_int,
    hid, dsilu, mixt, agg, up, wterm, rs_recv, z_src, z_recv, wfull,
    lsem, idx_s, idx_r, tab_s, tab_r, rs_s, rs_r, z_s, z_r, ag_s, ag_r, osem,
):
    n_nodes, feat = table.shape[1], table.shape[2]
    layers = wts.shape[0]
    blocks, per_row, tile, _ = itile.shape
    cap = n_nodes // owners
    share = feat // owners
    g = lax.axis_index("group")
    s = lax.axis_index("store")

    def peer(i):
        return lax.rem(s + i, owners)

    def zpeer(i):
        return lax.rem(g + i, groups)

    loads = [
        pltpu.make_async_copy(feat_hbm, table.at[0], lsem.at[0]),
        pltpu.make_async_copy(cnt_hbm, cnt, lsem.at[1]),
        pltpu.make_async_copy(iblk_hbm, iblk, lsem.at[2]),
        pltpu.make_async_copy(oblk_hbm, oblk, lsem.at[3]),
        pltpu.make_async_copy(itile_hbm, itile, lsem.at[4]),
        pltpu.make_async_copy(otile_hbm, otile, lsem.at[5]),
        pltpu.make_async_copy(past_h_hbm, table.at[pl.ds(1, 2)], lsem.at[6]),
        pltpu.make_async_copy(past_g_hbm, table.at[pl.ds(3, 2)], lsem.at[7]),
        pltpu.make_async_copy(w_hbm, wts, lsem.at[8]),
        pltpu.make_async_copy(cot_hbm, cot, lsem.at[9]),
    ]
    for load in loads:
        load.start()

    barrier = pltpu.get_barrier_semaphore()

    def greet_store(i, carry):
        pl.semaphore_signal(barrier, inc=1, device_id=(g, peer(i)), device_id_type=MESH)
        return carry

    def greet_group(i, carry):
        pl.semaphore_signal(barrier, inc=1, device_id=(zpeer(i), s), device_id_type=MESH)
        return carry

    lax.fori_loop(1, owners, greet_store, 0)
    lax.fori_loop(1, groups, greet_group, 0)

    for load in loads[1:6]:
        load.wait()
    lane = lax.broadcasted_iota(jnp.int32, (1, tile), 1)
    per_chunk = tile // cap

    def build(b, carry):
        in_tiles = [itile[b, k] for k in range(per_row)]
        in_tiles_t = [t.T for t in in_tiles]
        out_tiles = [otile[b, k] for k in range(per_row)]
        for c in range(blocks):
            live_to = jnp.zeros((1, tile), jnp.int32)
            for q in range(per_chunk):
                live_to = jnp.where(lane // cap == q, cnt[0, c * per_chunk + q], live_to)
            live = (lane % cap < live_to).astype(F32)
            din = jnp.zeros((tile, tile), BF)
            dint = jnp.zeros((tile, tile), BF)
            dout = jnp.zeros((tile, tile), BF)
            for k in range(per_row):
                keep = (jnp.full((1, tile), iblk[b, k], jnp.int32) == c).astype(F32).astype(BF)
                din = din + in_tiles[k] * keep
                dint = dint + in_tiles_t[k] * keep
                keep = (live * (jnp.full((1, tile), oblk[b, k], jnp.int32) == c).astype(F32)).astype(BF)
                dout = dout + out_tiles[k] * keep
            rows = pl.ds(pl.multiple_of(b * tile, tile), tile)
            a_in[rows, pl.ds(c * tile, tile)] = din
            a_out[rows, pl.ds(c * tile, tile)] = dout
            a_int[pl.ds(c * tile, tile), rows] = dint
        return carry

    lax.fori_loop(0, blocks, build, 0)

    pl.semaphore_wait(barrier, owners - 1 + groups - 1)

    def idx_copy(i):
        o = peer(i)
        first = pl.multiple_of(o * cap // tile * tile, tile)
        return pltpu.make_async_remote_copy(
            src_ref=rows_hbm.at[:, pl.ds(first, tile)],
            dst_ref=idx.at[pl.ds(s, 1)],
            send_sem=idx_s, recv_sem=idx_r, device_id=(g, o), device_id_type=MESH,
        )

    def idx_start(i, carry):
        idx_copy(i).start()
        return carry

    lax.fori_loop(1, owners, idx_start, 0)
    own_first = pl.multiple_of(s * cap // tile * tile, tile)
    own_idx = pltpu.make_async_copy(rows_hbm.at[:, pl.ds(own_first, tile)], idx.at[pl.ds(s, 1)], lsem.at[10])
    own_idx.start()
    own_idx.wait()
    for load in (loads[0],) + tuple(loads[6:]):
        load.wait()
    for sem in (idx_r, idx_s):
        pltpu.make_async_copy(idx.at[pl.ds(0, owners - 1)], idx.at[pl.ds(0, owners - 1)], sem).wait()

    wanted_f = idx[...].astype(F32)
    per_step = 4

    def make_onehot(step, carry):
        rows_here = per_step * cap
        part = idx[pl.ds(pl.multiple_of(step * per_step, per_step), per_step)].astype(F32)
        spread = jnp.broadcast_to(part[:, None, :], (per_step, cap, tile)).reshape(rows_here, tile)
        place = lax.broadcasted_iota(jnp.int32, (rows_here, tile), 0) % cap + lax.rem(s, per_chunk) * cap
        at = lax.broadcasted_iota(jnp.int32, (rows_here, tile), 1)
        col = jnp.sum(jnp.where(place == at, spread, 0.0), axis=1, keepdims=True)
        node = lax.broadcasted_iota(jnp.int32, (rows_here, n_nodes), 1).astype(F32)
        onehot[pl.ds(pl.multiple_of(step * rows_here, rows_here), rows_here)] = jnp.where(
            node == col, 1.0, 0.0
        ).astype(BF)
        return carry

    lax.fori_loop(0, owners // per_step, make_onehot, 0)

    own_rows = pl.ds(pl.multiple_of(s * cap, cap), cap)
    chunk = 256
    n_chunk = n_nodes // chunk

    def rows_of(m):
        return pl.ds(pl.multiple_of(m * chunk, chunk), chunk)

    def pull(t):
        def gather(m, carry):
            sendbuf[t, rows_of(m)] = dot(onehot[rows_of(m)], table[t]).astype(BF)
            return carry

        lax.fori_loop(0, n_chunk, gather, 0)

        def send(i, carry):
            o = peer(i)
            pltpu.make_async_remote_copy(
                src_ref=sendbuf.at[t, pl.ds(pl.multiple_of(o * cap, cap), cap)],
                dst_ref=recv.at[t, own_rows],
                send_sem=tab_s.at[t], recv_sem=tab_r.at[t], device_id=(g, o), device_id_type=MESH,
            ).start()
            return carry

        lax.fori_loop(1, owners, send, 0)
        recv[t, own_rows] = sendbuf[t, own_rows]

    def wait_table(sem, t):
        part = recv.at[t, pl.ds(0, n_nodes - cap)]
        pltpu.make_async_copy(part, part, sem.at[t]).wait()

    order = (0, 1, 2, 4, 3)
    for t in order:
        pull(t)

    outs = []

    for l in range(layers):
        beta = beta_of(l)
        wait_table(tab_r, l)

        def forward(m, carry, l=l, beta=beta):
            r = rows_of(m)
            h_now = table[0] if l == 0 else hid[l - 1]
            total = dot(a_in[r], h_now) + dot(a_out[r], recv[l])
            mixed = ((1.0 - RESTART) * total + RESTART * table[0, r].astype(F32)).astype(BF)
            pre = (1.0 - beta) * mixed.astype(F32) + beta * dot(mixed, wts[l])
            q = jax.nn.sigmoid(pre)
            hid[l, r] = (pre * q).astype(BF)
            dsilu[l, r] = q * (1.0 + pre * (1.0 - q))
            mixt[l, :, r] = mixed.T
            return carry

        lax.fori_loop(0, n_chunk, forward, 0)
        outs.append(pltpu.make_async_copy(hid.at[l], hid_hbm.at[l], osem.at[l]))
        outs[-1].start()

    def rs_start(l):
        def go(i, carry):
            o = peer(i)
            pltpu.make_async_remote_copy(
                src_ref=wterm.at[l, pl.ds(pl.multiple_of(o * share, share), share)],
                dst_ref=rs_recv.at[l, pl.ds(pl.multiple_of(s * share, share), share)],
                send_sem=rs_s.at[l], recv_sem=rs_r.at[l], device_id=(g, o), device_id_type=MESH,
            ).start()
            return carry

        lax.fori_loop(1, owners, go, 0)
        own = pl.ds(pl.multiple_of(s * share, share), share)
        rs_recv[l, own] = wterm[l, own]

    def rs_end(l):
        part = rs_recv.at[l, pl.ds(0, feat - share)]
        pltpu.make_async_copy(part, part, rs_r.at[l]).wait()
        z_src[l] = jnp.sum(rs_recv[l].reshape(owners, share, feat), axis=0)

    def z_start(l):
        def go(i, carry):
            pltpu.make_async_remote_copy(
                src_ref=z_src.at[l], dst_ref=z_recv.at[l, pl.ds(pl.multiple_of(g * share, share), share)],
                send_sem=z_s.at[l], recv_sem=z_r.at[l], device_id=(zpeer(i), s), device_id_type=MESH,
            ).start()
            return carry

        lax.fori_loop(1, groups, go, 0)
        z_recv[l, pl.ds(pl.multiple_of(g * share, share), share)] = z_src[l]

    def z_end(l):
        part = z_recv.at[l, pl.ds(0, (groups - 1) * share)]
        pltpu.make_async_copy(part, part, z_r.at[l]).wait()
        total = jnp.sum(z_recv[l].reshape(groups, share, feat), axis=0)
        own = pl.ds(pl.multiple_of(s * share, share), share)
        wfull[l, own] = total * (beta_of(l) / math.sqrt(node_total))

    def ag_start(l):
        own = pl.ds(pl.multiple_of(s * share, share), share)

        def go(i, carry):
            pltpu.make_async_remote_copy(
                src_ref=wfull.at[l, own], dst_ref=wfull.at[l, own],
                send_sem=ag_s.at[l], recv_sem=ag_r.at[l], device_id=(g, peer(i)), device_id_type=MESH,
            ).start()
            return carry

        lax.fori_loop(1, owners, go, 0)

    def ag_end(l):
        part = wfull.at[l, pl.ds(0, feat - share)]
        pltpu.make_async_copy(part, part, ag_r.at[l]).wait()

    for l in reversed(range(layers)):
        beta = beta_of(l)
        if l == layers - 1:
            def first_up(m, carry):
                up[rows_of(m)] = cot[rows_of(m)].astype(F32)
                return carry

            lax.fori_loop(0, n_chunk, first_up, 0)
        else:
            src = l

            def inner_part(m, carry, src=src):
                up[rows_of(m)] = dot(a_int[rows_of(m)], agg[src])
                return carry

            lax.fori_loop(0, n_chunk, inner_part, 0)
            wait_table(tab_r, 3 + src)

            def outer_part(m, carry, src=src):
                up[rows_of(m)] += dot(a_out[rows_of(m)], recv[3 + src])
                return carry

            lax.fori_loop(0, n_chunk, outer_part, 0)

        wterm[l] = jnp.zeros((feat, feat), F32)

        def backward(m, carry, l=l, beta=beta):
            r = rows_of(m)
            pg = (up[r] * dsilu[l, r]).astype(BF)
            wterm[l] += dot(mixt[l, :, r], pg)
            if l >= 1:
                mix = (1.0 - beta) * pg.astype(F32) + beta * dot_nt(pg, wts[l])
                agg[l - 1, r] = ((1.0 - RESTART) * mix).astype(BF)
            return carry

        lax.fori_loop(0, n_chunk, backward, 0)
        rs_start(l)
        if l >= 1:
            outs.append(pltpu.make_async_copy(agg.at[l - 1], gout_hbm.at[l - 1], osem.at[layers + l - 1]))
            outs[-1].start()

    down = tuple(reversed(range(layers)))
    for l in down:
        rs_end(l)
        z_start(l)
    for l in down:
        z_end(l)
        ag_start(l)
    for l in down:
        ag_end(l)
    last = pltpu.make_async_copy(wfull, wg_hbm, osem.at[2 * layers - 1])
    last.start()

    for t in order:
        wait_table(tab_s, t)
    for l in down:
        for ref, sem, n in ((rs_recv, rs_s, feat - share), (z_recv, z_s, (groups - 1) * share), (wfull, ag_s, feat - share)):
            part = ref.at[l, pl.ds(0, n)]
            pltpu.make_async_copy(part, part, sem.at[l]).wait()
    for out in outs:
        out.wait()
    last.wait()


def per_device(features, past_hidden, past_grads, cotangent, weights, inner_tiles, inner_blocks,
               outer_tiles, outer_blocks, slot_rows, slot_counts):
    owners = lax.axis_size("store")
    groups = lax.axis_size("group")
    nodes, feat = features.shape
    layers = weights.shape[0]
    blocks, per_row, tile, _ = inner_tiles.shape
    node_total = nodes * owners * groups
    share = feat // owners
    anyspec = pl.BlockSpec(memory_space=pl.ANY)
    V = pltpu.VMEM
    S = pltpu.SemaphoreType.DMA
    return pl.pallas_call(
        functools.partial(step_kernel, groups, owners, node_total),
        out_shape=(
            jax.ShapeDtypeStruct((layers, nodes, feat), BF),
            jax.ShapeDtypeStruct((layers - 1, nodes, feat), BF),
            jax.ShapeDtypeStruct((layers, feat, feat), F32),
        ),
        in_specs=[anyspec] * 11,
        out_specs=(anyspec,) * 3,
        scratch_shapes=[
            V((5, nodes, feat), BF),
            V((nodes, feat), BF),
            V((layers, feat, feat), BF),
            V((blocks, per_row, tile, tile), BF),
            V((blocks, per_row, tile, tile), BF),
            pltpu.SMEM((blocks, per_row), jnp.int32),
            pltpu.SMEM((blocks, per_row), jnp.int32),
            pltpu.SMEM((1, owners), jnp.int32),
            V((owners, tile), jnp.int32),
            V((nodes, nodes), BF),
            V((5, nodes, feat), BF),
            V((5, nodes, feat), BF),
            V((nodes, nodes), BF),
            V((nodes, nodes), BF),
            V((nodes, nodes), BF),
            V((layers, nodes, feat), BF),
            V((layers, nodes, feat), F32),
            V((layers, feat, nodes), BF),
            V((layers - 1, nodes, feat), BF),
            V((nodes, feat), F32),
            V((layers, feat, feat), F32),
            V((layers, feat, feat), F32),
            V((layers, share, feat), F32),
            V((layers, groups * share, feat), F32),
            V((layers, feat, feat), F32),
            S((11,)), S, S, S((5,)), S((5,)),
            S((layers,)), S((layers,)), S((layers,)), S((layers,)), S((layers,)), S((layers,)),
            S((2 * layers,)),
        ],
        compiler_params=pltpu.CompilerParams(
            collective_id=0, has_side_effects=True, vmem_limit_bytes=56 << 20
        ),
        name="lmc_step",
    )(features, past_hidden, past_grads, cotangent, weights, inner_tiles, inner_blocks,
      outer_tiles, outer_blocks, slot_rows, slot_counts)


def solution(mesh):
    placed = (
        P(("group", "store"), None),
        P(None, ("group", "store"), None),
        P(None, ("group", "store"), None),
        P(("group", "store"), None),
        P(),
        P(("group", "store"), None, None, None),
        P(("group", "store"), None),
        P(("group", "store"), None, None, None),
        P(("group", "store"), None),
        P(("group", "store"), None),
        P(("group", "store"), None),
    )
    return jax.shard_map(
        per_device,
        mesh=mesh,
        in_specs=placed,
        out_specs=(P(None, ("group", "store"), None), P(None, ("group", "store"), None), P()),
        check_vma=False,
    )
```

```python
import functools
import math

import jax
import jax.numpy as jnp
from jax import lax
from jax.experimental import pallas as pl
from jax.experimental.pallas import tpu as pltpu
from jax.sharding import PartitionSpec as P

RESTART = 0.1
MESH = pl.DeviceIdType.MESH
BF = jnp.bfloat16
F32 = jnp.float32


def beta_of(layer_idx):
    return math.log(0.5 / (layer_idx + 1) + 1.0)


def dot(lhs, rhs):
    return jnp.dot(lhs, rhs, preferred_element_type=F32)


def dot_nt(lhs, rhs):
    return lax.dot_general(lhs, rhs, (((1,), (1,)), ((), ())), preferred_element_type=F32)


def step_kernel(
    groups, owners, node_total,
    feat_hbm, past_h_hbm, past_g_hbm, cot_hbm, w_hbm, itile_hbm, iblk_hbm, otile_hbm, oblk_hbm,
    rows_hbm, cnt_hbm,
    hid, agg, wfull,
    table, cot, wts, itile, otile, iblk, oblk, cnt, rows, idx,
    onehot, sendbuf, recv, a_in, a_out, a_int, dsilu, mixt, up,
    wterm, core_recv, reduced, rs_recv, z_src, z_recv, wag,
    lsem, idx_s, idx_r, tab_s, tab_r, core_s, core_r, rs_s, rs_r, z_s, z_r, ag_s, ag_r,
):
    n_nodes, feat = table.shape[1], table.shape[2]
    layers = wts.shape[0]
    blocks, per_row, tile, _ = itile.shape
    cap = n_nodes // owners
    chips = owners // 2
    side = 4
    half = feat // 2
    share = feat // chips
    g = lax.axis_index("group")
    s = lax.axis_index("store")
    chip, core = s // 2, lax.rem(s, 2)
    cx, cy = chip // side, lax.rem(chip, side)

    def spread(j):
        return jnp.where(j == 0, 2, jnp.where(j == 1, 1, jnp.where(j == 2, 3, 0)))

    def chip_peer(j):
        return lax.rem(cx + spread(j // side), side) * side + lax.rem(cy + spread(lax.rem(j, side)), side)

    def peer(i):
        return chip_peer(i // 2) * 2 + lax.rem(core + 1 + lax.rem(i, 2), 2)

    def zpeer(i):
        mid = groups // 2
        return lax.rem(g + jnp.where(lax.rem(i, 2) == 0, mid + i // 2, mid - (i + 1) // 2), groups)

    ring = (2, 1, 3, 0)
    x_rows = [lax.rem(cx + a, side) for a in ring]
    steps = sorted(
        ((a, b, c) for a in range(side) for b in range(side) for c in range(2) if (a, b, c) != (0, 0, 0)),
        key=lambda p: -min(p[0], side - p[0]) - min(p[1], side - p[1]),
    )
    far = [
        (lax.rem(cx + a, side) * side + lax.rem(cy + b, side)) * 2 + lax.rem(core + c, 2) for a, b, c in steps
    ]
    far_chips = [
        lax.rem(cx + a, side) * side + lax.rem(cy + b, side) for a, b, c in steps if c == 0
    ]

    def each(count, act):
        def step(i, carry):
            act(i)
            return carry

        lax.fori_loop(0, count, step, 0)

    def block(index, size):
        return pl.ds(pl.multiple_of(index * size, size), size)

    def push(src, dst, send_sem, recv_sem, group, store):
        pltpu.make_async_remote_copy(
            src_ref=src, dst_ref=dst, send_sem=send_sem, recv_sem=recv_sem,
            device_id=(group, store), device_id_type=MESH,
        ).start()

    def drain(part, *sems):
        for sem in sems:
            pltpu.make_async_copy(part, part, sem).wait()

    loads = [
        pltpu.make_async_copy(src, dst, lsem.at[i])
        for i, (src, dst) in enumerate((
            (rows_hbm, rows),
            (cnt_hbm, cnt),
            (iblk_hbm, iblk),
            (oblk_hbm, oblk),
            (itile_hbm, itile),
            (otile_hbm, otile),
            (feat_hbm, table.at[0]),
            (past_h_hbm, table.at[pl.ds(1, 2)]),
            (past_g_hbm.at[1], table.at[3]),
            (past_g_hbm.at[0], table.at[4]),
            (w_hbm, wts),
            (cot_hbm, cot),
        ))
    ]
    for load in loads:
        load.start()

    barrier = pltpu.get_barrier_semaphore()
    each(owners - 1, lambda i: pl.semaphore_signal(
        barrier, inc=1, device_id=(g, peer(i)), device_id_type=MESH))
    each(groups - 1, lambda i: pl.semaphore_signal(
        barrier, inc=1, device_id=(zpeer(i), s), device_id_type=MESH))
    loads[0].wait()
    pl.semaphore_wait(barrier, owners - 1 + groups - 1)

    def wanted_lanes(o):
        return rows.at[:, pl.ds(pl.multiple_of(o * cap // tile * tile, tile), tile)]

    for o in far:
        push(wanted_lanes(o), idx.at[pl.ds(s, 1)], idx_s, idx_r, g, o)

    own_idx = pltpu.make_async_copy(wanted_lanes(s), idx.at[pl.ds(s, 1)], lsem.at[12])
    own_idx.start()

    for load in loads[1:6]:
        load.wait()
    lane = lax.broadcasted_iota(jnp.int32, (1, tile), 1)
    per_chunk = tile // cap

    def build(b):
        in_tiles = [itile[b, k] for k in range(per_row)]
        in_tiles_t = [t.T for t in in_tiles]
        out_tiles = [otile[b, k] for k in range(per_row)]
        for c in range(blocks):
            live_to = jnp.zeros((1, tile), jnp.int32)
            for q in range(per_chunk):
                live_to = jnp.where(lane // cap == q, cnt[0, c * per_chunk + q], live_to)
            live = (lane % cap < live_to).astype(F32)
            din = jnp.zeros((tile, tile), BF)
            dint = jnp.zeros((tile, tile), BF)
            dout = jnp.zeros((tile, tile), BF)
            for k in range(per_row):
                keep = (jnp.full((1, tile), iblk[k, b], jnp.int32) == c).astype(F32).astype(BF)
                din = din + in_tiles[k] * keep
                dint = dint + in_tiles_t[k] * keep
                keep = (live * (jnp.full((1, tile), oblk[k, b], jnp.int32) == c).astype(F32)).astype(BF)
                dout = dout + out_tiles[k] * keep
            here = block(b, tile)
            a_in[here, pl.ds(c * tile, tile)] = din
            a_out[here, pl.ds(c * tile, tile)] = dout
            a_int[pl.ds(c * tile, tile), here] = dint

    each(blocks, build)
    own_idx.wait()
    for load in loads[6:]:
        load.wait()
    drain(idx.at[pl.ds(0, owners - 1)], idx_r, idx_s)

    chunk = n_nodes // side
    n_chunk = side
    per_quarter = owners // side

    def make_onehot(quarter):
        part = idx[block(quarter, per_quarter)].astype(F32)
        wide = jnp.broadcast_to(part[:, None, :], (per_quarter, cap, tile)).reshape(chunk, tile)
        place = lax.broadcasted_iota(jnp.int32, (chunk, tile), 0) % cap + lax.rem(s, per_chunk) * cap
        at = lax.broadcasted_iota(jnp.int32, (chunk, tile), 1)
        col = jnp.sum(jnp.where(place == at, wide, 0.0), axis=1, keepdims=True)
        node = lax.broadcasted_iota(jnp.int32, (chunk, n_nodes), 1).astype(F32)
        hot = jnp.where(node == col, 1.0, 0.0).astype(BF)
        onehot[block(quarter, chunk)] = hot
        return hot

    def send_rows(t, o):
        push(sendbuf.at[t, block(o, cap)], recv.at[t, block(s, cap)], tab_s.at[t], tab_r.at[t], g, o)

    def gather(t, quarter, hot):
        sendbuf[t, block(quarter, chunk)] = dot(hot, table[t]).astype(BF)

    for j in range(side):
        gather(0, x_rows[j], make_onehot(x_rows[j]))
    for o in far:
        send_rows(0, o)
    recv[0, block(s, cap)] = sendbuf[0, block(s, cap)]

    def pull_next(t):
        t = t + 1
        for quarter in range(side):
            gather(t, quarter, onehot[block(quarter, chunk)])
        for o in far:
            send_rows(t, o)
        recv[t, block(s, cap)] = sendbuf[t, block(s, cap)]

    each(table.shape[0] - 1, pull_next)

    def arrived(t):
        drain(recv.at[t, pl.ds(0, n_nodes - cap)], tab_r.at[t])

    for l in range(layers):
        beta = beta_of(l)
        arrived(l)

        def forward(m, l=l, beta=beta):
            r = block(m, chunk)
            h_now = table[0] if l == 0 else hid[l - 1]
            total = dot(a_in[r], h_now) + dot(a_out[r], recv[l])
            mixed = ((1.0 - RESTART) * total + RESTART * table[0, r].astype(F32)).astype(BF)
            pre = (1.0 - beta) * mixed.astype(F32) + beta * dot(mixed, wts[l])
            q = jax.nn.sigmoid(pre)
            hid[l, r] = (pre * q).astype(BF)
            dsilu[l, r] = q * (1.0 + pre * (1.0 - q))
            mixt[l, :, r] = mixed.T

        each(n_chunk, forward)

    def core_start(l):
        push(wterm.at[l, 1 - core], core_recv.at[l], core_s.at[l], core_r.at[l], g, chip * 2 + 1 - core)

    def core_end(l):
        drain(core_recv.at[l], core_r.at[l])
        reduced[l] = wterm[l, core] + core_recv[l]

    def rs_start(l):
        def go(k):
            push(reduced.at[l, block(k, share)], rs_recv.at[l, block(chip, share)],
                 rs_s.at[l], rs_r.at[l], g, k * 2 + core)

        if l == 0:
            for k in far_chips:
                go(k)
        else:
            each(chips - 1, lambda j: go(chip_peer(j)))
        rs_recv[l, block(chip, share)] = reduced[l, block(chip, share)]

    def rs_end(l):
        drain(rs_recv.at[l, pl.ds(0, feat - share)], rs_r.at[l])
        z_src[l] = jnp.sum(rs_recv[l].reshape(chips, share, half), axis=0)

    def z_start(l):
        each(groups - 1, lambda i: push(
            z_src.at[l], z_recv.at[l, block(g, share)], z_s.at[l], z_r.at[l], zpeer(i), s))
        z_recv[l, block(g, share)] = z_src[l]

    def z_end(l):
        drain(z_recv.at[l, pl.ds(0, (groups - 1) * share)], z_r.at[l])
        total = jnp.sum(z_recv[l].reshape(groups, share, half), axis=0)
        wag[l, block(core * chips + chip, share)] = (
            total * (beta_of(l) / math.sqrt(node_total))).astype(BF)

    def ag_start(l):
        own = block(core * chips + chip, share)

        def go(o):
            push(wag.at[l, own], wag.at[l, own], ag_s.at[l], ag_r.at[l], g, o)

        if l == 0:
            for o in far:
                go(o)
        else:
            each(owners - 1, lambda i: go(peer(i)))

    def ag_end(l):
        drain(wag.at[l, pl.ds(0, 2 * feat - share)], ag_r.at[l])
        for c in range(2):
            wfull[l, :, c * half:(c + 1) * half] = wag[l, c * feat:(c + 1) * feat].astype(F32)

    for l in reversed(range(layers)):
        beta = beta_of(l)
        if l < layers - 1:
            def inner_part(m, l=l):
                up[block(m, chunk)] = dot(a_int[block(m, chunk)], agg[l])

            each(n_chunk, inner_part)
            core_end(l + 1)
            rs_start(l + 1)
            t = 2 * layers - 2 - l
            arrived(t)
        wsum = [None, None]
        for m in range(n_chunk):
            r = pl.ds(m * chunk, chunk)
            if l == layers - 1:
                above = cot[r].astype(F32)
            else:
                above = up[r] + dot(a_out[r], recv[t])
            pg = (above * dsilu[l, r]).astype(BF)
            part = dot(mixt[l, :, r], pg)
            for c in range(2):
                cols = part[:, c * half:(c + 1) * half]
                wsum[c] = cols if m == 0 else wsum[c] + cols
            if l >= 1:
                mix = (1.0 - beta) * pg.astype(F32) + beta * dot_nt(pg, wts[l])
                agg[l - 1, r] = ((1.0 - RESTART) * mix).astype(BF)
        for c in range(2):
            wterm[l, c] = wsum[c]
        core_start(l)

    down = tuple(reversed(range(layers)))
    core_end(0)
    rs_start(0)
    for l in down:
        rs_end(l)
        z_start(l)
    for l in down:
        z_end(l)
        ag_start(l)
    for l in down:
        ag_end(l)

    for t in range(table.shape[0]):
        drain(recv.at[t, pl.ds(0, n_nodes - cap)], tab_s.at[t])
    for l in down:
        drain(core_recv.at[l], core_s.at[l])
        drain(rs_recv.at[l, pl.ds(0, feat - share)], rs_s.at[l])
        drain(z_recv.at[l, pl.ds(0, (groups - 1) * share)], z_s.at[l])
        drain(wag.at[l, pl.ds(0, 2 * feat - share)], ag_s.at[l])


def store_kernel(hid, agg, wfull, hid_hbm, agg_hbm, wg_hbm, sem):
    copies = [
        pltpu.make_async_copy(src, dst, sem.at[i])
        for i, (src, dst) in enumerate(((hid, hid_hbm), (agg, agg_hbm), (wfull, wg_hbm)))
    ]
    for copy in copies:
        copy.start()
    for copy in copies:
        copy.wait()


def per_device(features, past_hidden, past_grads, cotangent, weights, inner_tiles, inner_blocks,
               outer_tiles, outer_blocks, slot_rows, slot_counts):
    owners = lax.axis_size("store")
    groups = lax.axis_size("group")
    nodes, feat = features.shape
    layers = weights.shape[0]
    blocks, per_row, tile, _ = inner_tiles.shape
    node_total = nodes * owners * groups
    share = feat // (owners // 2)
    anyspec = pl.BlockSpec(memory_space=pltpu.HBM)
    V = pltpu.VMEM
    S = pltpu.SemaphoreType.DMA
    res = pl.pallas_call(
        functools.partial(step_kernel, groups, owners, node_total),
        out_shape=(
            V((layers, nodes, feat), BF),
            V((layers - 1, nodes, feat), BF),
            V((layers, feat, feat), F32),
        ),
        in_specs=[anyspec] * 11,
        out_specs=(pl.BlockSpec(memory_space=V),) * 3,
        scratch_shapes=[
            V((5, nodes, feat), BF),
            V((nodes, feat), BF),
            V((layers, feat, feat), BF),
            V((blocks, per_row, tile, tile), BF),
            V((blocks, per_row, tile, tile), BF),
            pltpu.SMEM((per_row, blocks), jnp.int32),
            pltpu.SMEM((per_row, blocks), jnp.int32),
            pltpu.SMEM((1, owners), jnp.int32),
            V((1, nodes), jnp.int32),
            V((owners, tile), jnp.int32),
            V((nodes, nodes), BF),
            V((5, nodes, feat), BF),
            V((5, nodes, feat), BF),
            V((nodes, nodes), BF),
            V((nodes, nodes), BF),
            V((nodes, nodes), BF),
            V((layers, nodes, feat), F32),
            V((layers, feat, nodes), BF),
            V((nodes, feat), F32),
            V((layers, 2, feat, feat // 2), F32),
            V((layers, feat, feat // 2), F32),
            V((layers, feat, feat // 2), F32),
            V((layers, feat, feat // 2), F32),
            V((layers, share, feat // 2), F32),
            V((layers, groups * share, feat // 2), F32),
            V((layers, 2 * feat, feat // 2), BF),
            S((13,)), S, S, S((5,)), S((5,)),
            S((layers,)), S((layers,)), S((layers,)), S((layers,)),
            S((layers,)), S((layers,)), S((layers,)), S((layers,)),
        ],
        compiler_params=pltpu.CompilerParams(
            collective_id=0, has_side_effects=True, vmem_limit_bytes=60 << 20
        ),
        name="lmc_step",
    )(features, past_hidden, past_grads, cotangent, weights, inner_tiles, inner_blocks.T,
      outer_tiles, outer_blocks.T, slot_rows, slot_counts)
    return pl.pallas_call(
        store_kernel,
        out_shape=tuple(jax.ShapeDtypeStruct(r.shape, r.dtype) for r in res),
        in_specs=[pl.BlockSpec(memory_space=V)] * 3,
        out_specs=(anyspec,) * 3,
        scratch_shapes=[S((3,))],
        compiler_params=pltpu.CompilerParams(vmem_limit_bytes=1 << 20),
        name="store_results",
    )(*[pltpu.with_memory_space_constraint(r, V) for r in res])


def solution(mesh):
    placed = (
        P(("group", "store"), None),
        P(None, ("group", "store"), None),
        P(None, ("group", "store"), None),
        P(("group", "store"), None),
        P(),
        P(("group", "store"), None, None, None),
        P(("group", "store"), None),
        P(("group", "store"), None, None, None),
        P(("group", "store"), None),
        P(("group", "store"), None),
        P(("group", "store"), None),
    )
    return jax.shard_map(
        per_device,
        mesh=mesh,
        in_specs=placed,
        out_specs=(P(None, ("group", "store"), None), P(None, ("group", "store"), None), P()),
        check_vma=False,
    )
```

```python
import functools
import math

import jax
import jax.numpy as jnp
from jax import lax
from jax.experimental import pallas as pl
from jax.experimental.pallas import tpu as pltpu
from jax.sharding import PartitionSpec as P

RESTART = 0.1
MESH = pl.DeviceIdType.MESH
BF = jnp.bfloat16
F32 = jnp.float32


def beta_of(layer_idx):
    return math.log(0.5 / (layer_idx + 1) + 1.0)


def dot(lhs, rhs):
    return jnp.dot(lhs, rhs, preferred_element_type=F32)


def dot_nt(lhs, rhs):
    return lax.dot_general(lhs, rhs, (((1,), (1,)), ((), ())), preferred_element_type=F32)


def step_kernel(
    groups, owners, node_total,
    feat_hbm, past_h_hbm, past_g_hbm, cot_hbm, w_hbm, itile_hbm, iblk_hbm, otile_hbm, oblk_hbm,
    rows_hbm, cnt_hbm,
    hid, agg, wfull,
    table, cot, wts, itile, otile, iblk, oblk, cnt, rows, idx,
    onehot, sendbuf, recv, a_in, a_out, a_int, dsilu, mixt, mixed_last, pgs, up,
    wterm, core_recv, reduced, rs_recv, z_src, z_recv, wag,
    lsem, idx_s, idx_r, tab_s, tab_r, core_s, core_r, rs_s, rs_r, z_s, z_r, ag_s, ag_r,
):
    n_nodes, feat = table.shape[1], table.shape[2]
    layers = wts.shape[0]
    blocks, per_row, tile, _ = itile.shape
    cap = n_nodes // owners
    chips = owners // 2
    side = 4
    half = feat // 2
    share = feat // chips
    g = lax.axis_index("group")
    s = lax.axis_index("store")
    chip, core = s // 2, lax.rem(s, 2)
    cx, cy = chip // side, lax.rem(chip, side)

    def spread(j):
        return jnp.where(j == 0, 2, jnp.where(j == 1, 1, jnp.where(j == 2, 3, 0)))

    def chip_peer(j):
        return lax.rem(cx + spread(j // side), side) * side + lax.rem(cy + spread(lax.rem(j, side)), side)

    def peer(i):
        return chip_peer(i // 2) * 2 + lax.rem(core + 1 + lax.rem(i, 2), 2)

    def zpeer(i):
        mid = groups // 2
        return lax.rem(g + jnp.where(lax.rem(i, 2) == 0, mid + i // 2, mid - (i + 1) // 2), groups)

    ring = (2, 1, 3, 0)
    x_rows = [lax.rem(cx + a, side) for a in ring]
    steps = sorted(
        ((a, b, c) for a in range(side) for b in range(side) for c in range(2) if (a, b, c) != (0, 0, 0)),
        key=lambda p: (-min(p[0], side - p[0]) - min(p[1], side - p[1]), p[2], (p[0] + 2 * p[1]) % 4, p),
    )
    far = [
        (lax.rem(cx + a, side) * side + lax.rem(cy + b, side)) * 2 + lax.rem(core + c, 2) for a, b, c in steps
    ]
    far_chips = [
        lax.rem(cx + a, side) * side + lax.rem(cy + b, side) for a, b, c in steps if c == 0
    ]

    def each(count, act):
        def step(i, carry):
            act(i)
            return carry

        lax.fori_loop(0, count, step, 0)

    def block(index, size):
        return pl.ds(pl.multiple_of(index * size, size), size)

    def push(src, dst, send_sem, recv_sem, group, store):
        pltpu.make_async_remote_copy(
            src_ref=src, dst_ref=dst, send_sem=send_sem, recv_sem=recv_sem,
            device_id=(group, store), device_id_type=MESH,
        ).start()

    def drain(part, *sems):
        for sem in sems:
            pltpu.make_async_copy(part, part, sem).wait()

    loads = [
        pltpu.make_async_copy(src, dst, lsem.at[i])
        for i, (src, dst) in enumerate((
            (rows_hbm, rows),
            (cnt_hbm, cnt),
            (iblk_hbm, iblk),
            (oblk_hbm, oblk),
            (itile_hbm, itile),
            (otile_hbm, otile),
            (feat_hbm, table.at[0]),
            (past_h_hbm, table.at[pl.ds(1, 2)]),
            (past_g_hbm.at[1], table.at[3]),
            (past_g_hbm.at[0], table.at[4]),
            (w_hbm, wts),
            (cot_hbm, cot),
        ))
    ]
    loads[0].start()

    barrier = pltpu.get_barrier_semaphore()
    each(groups - 1, lambda i: pl.semaphore_signal(
        barrier, inc=1, device_id=(zpeer(i), s), device_id_type=MESH))
    for o in far:
        pl.semaphore_signal(barrier, inc=1, device_id=(g, o), device_id_type=MESH)
    for load in loads[1:]:
        load.start()
    loads[0].wait()
    pl.semaphore_wait(barrier, owners - 1 + groups - 1)

    def wanted_lanes(o):
        return rows.at[:, pl.ds(pl.multiple_of(o * cap // tile * tile, tile), tile)]

    for o in far:
        push(wanted_lanes(o), idx.at[pl.ds(s, 1)], idx_s, idx_r, g, o)

    own_idx = pltpu.make_async_copy(wanted_lanes(s), idx.at[pl.ds(s, 1)], lsem.at[12])
    own_idx.start()

    for load in loads[1:6]:
        load.wait()
    lane = lax.broadcasted_iota(jnp.int32, (1, tile), 1)
    per_chunk = tile // cap

    def build(b):
        in_tiles = [itile[b, k] for k in range(per_row)]
        in_tiles_t = [t.T for t in in_tiles]
        out_tiles = [otile[b, k] for k in range(per_row)]
        for c in range(blocks):
            live_to = jnp.zeros((1, tile), jnp.int32)
            for q in range(per_chunk):
                live_to = jnp.where(lane // cap == q, cnt[0, c * per_chunk + q], live_to)
            live = (lane % cap < live_to).astype(F32)
            din = jnp.zeros((tile, tile), BF)
            dint = jnp.zeros((tile, tile), BF)
            dout = jnp.zeros((tile, tile), BF)
            for k in range(per_row):
                keep = (jnp.full((1, tile), iblk[k, b], jnp.int32) == c).astype(F32).astype(BF)
                din = din + in_tiles[k] * keep
                dint = dint + in_tiles_t[k] * keep
                keep = (live * (jnp.full((1, tile), oblk[k, b], jnp.int32) == c).astype(F32)).astype(BF)
                dout = dout + out_tiles[k] * keep
            here = block(b, tile)
            a_in[here, pl.ds(c * tile, tile)] = din
            a_out[here, pl.ds(c * tile, tile)] = dout
            a_int[pl.ds(c * tile, tile), here] = dint

    each(blocks, build)
    own_idx.wait()
    for load in loads[6:]:
        load.wait()
    drain(idx.at[pl.ds(0, owners - 1)], idx_r, idx_s)

    chunk = n_nodes // side
    n_chunk = side
    per_quarter = owners // side

    ranked = far + [s]

    def make_onehot(quarter):
        asked = [idx[pl.ds(o, 1)] for o in ranked[quarter * per_quarter:(quarter + 1) * per_quarter]]
        part = jnp.concatenate(asked, axis=0).astype(F32)
        wide = jnp.broadcast_to(part[:, None, :], (per_quarter, cap, tile)).reshape(chunk, tile)
        place = lax.broadcasted_iota(jnp.int32, (chunk, tile), 0) % cap + lax.rem(s, per_chunk) * cap
        at = lax.broadcasted_iota(jnp.int32, (chunk, tile), 1)
        col = jnp.sum(jnp.where(place == at, wide, 0.0), axis=1, keepdims=True)
        node = lax.broadcasted_iota(jnp.int32, (chunk, n_nodes), 1).astype(F32)
        hot = jnp.where(node == col, 1.0, 0.0).astype(BF)
        onehot[pl.ds(quarter * chunk, chunk)] = hot
        return hot

    def pull(t, hot_of):
        for quarter in range(side):
            first = quarter * per_quarter
            sendbuf[t, pl.ds(quarter * chunk, chunk)] = dot(hot_of(quarter), table[t]).astype(BF)
            for i in range(first, first + per_quarter):
                if i < owners - 1:
                    push(sendbuf.at[t, pl.ds(i * cap, cap)], recv.at[t, block(s, cap)],
                         tab_s.at[t], tab_r.at[t], g, ranked[i])
        recv[t, block(s, cap)] = sendbuf[t, pl.ds((owners - 1) * cap, cap)]

    pull(0, make_onehot)
    each(table.shape[0] - 1, lambda t: pull(t + 1, lambda quarter: onehot[pl.ds(quarter * chunk, chunk)]))

    def arrived(t):
        drain(recv.at[t, pl.ds(0, n_nodes - cap)], tab_r.at[t])

    for l in range(layers):
        beta = beta_of(l)
        arrived(l)

        def forward(m, l=l, beta=beta):
            r = pl.ds(m * chunk, chunk)
            h_now = table[0] if l == 0 else hid[l - 1]
            total = dot(a_in[r], h_now) + dot(a_out[r], recv[l])
            mixed = ((1.0 - RESTART) * total + RESTART * table[0, r].astype(F32)).astype(BF)
            pre = (1.0 - beta) * mixed.astype(F32) + beta * dot(mixed, wts[l])
            q = jax.nn.sigmoid(pre)
            act = pre * q
            hid[l, r] = act.astype(BF)
            dsilu[l, r] = q + act * (1.0 - q)
            if l < layers - 1:
                mixt[l, :, r] = mixed.T
            else:
                mixed_last[r] = mixed

        for m in range(n_chunk):
            forward(m)

    def core_start(l):
        push(wterm.at[l, 1 - core], core_recv.at[l], core_s.at[l], core_r.at[l], g, chip * 2 + 1 - core)

    def core_end(l):
        drain(core_recv.at[l], core_r.at[l])
        reduced[l] = wterm[l, core] + core_recv[l]

    def rs_start(l):
        def go(k):
            push(reduced.at[l, block(k, share)], rs_recv.at[l, block(chip, share)],
                 rs_s.at[l], rs_r.at[l], g, k * 2 + core)

        if l == 0:
            for k in far_chips:
                go(k)
        else:
            each(chips - 1, lambda j: go(chip_peer(j)))
        rs_recv[l, block(chip, share)] = reduced[l, block(chip, share)]

    def rs_end(l):
        drain(rs_recv.at[l, pl.ds(0, feat - share)], rs_r.at[l])
        z_src[l] = jnp.sum(rs_recv[l].reshape(chips, share, half), axis=0)

    def z_start(l):
        each(groups - 1, lambda i: push(
            z_src.at[l], z_recv.at[l, block(g, share)], z_s.at[l], z_r.at[l], zpeer(i), s))
        z_recv[l, block(g, share)] = z_src[l]

    def z_end(l):
        drain(z_recv.at[l, pl.ds(0, (groups - 1) * share)], z_r.at[l])
        total = jnp.sum(z_recv[l].reshape(groups, share, half), axis=0)
        wag[l, block(core * chips + chip, share)] = (
            total * (beta_of(l) / math.sqrt(node_total))).astype(BF)

    def ag_start(l):
        own = block(core * chips + chip, share)

        def go(o):
            push(wag.at[l, own], wag.at[l, own], ag_s.at[l], ag_r.at[l], g, o)

        if l == 0:
            for o in far:
                go(o)
        else:
            each(owners - 1, lambda i: go(peer(i)))

    def ag_end(l):
        drain(wag.at[l, pl.ds(0, 2 * feat - share)], ag_r.at[l])
        for c in range(2):
            wfull[l, :, c * half:(c + 1) * half] = wag[l, c * feat:(c + 1) * feat].astype(F32)

    def weight_term(l, pgs):
        wsum = [None, None]
        for m, pg in enumerate(pgs):
            r = pl.ds(m * chunk, chunk)
            part = dot(mixt[l, :, r], pg)
            for c in range(2):
                cols = part[:, c * half:(c + 1) * half]
                wsum[c] = cols if m == 0 else wsum[c] + cols
        for c in range(2):
            wterm[l, c] = wsum[c]
        core_start(l)

    for l in reversed(range(layers)):
        beta = beta_of(l)
        if l < layers - 1:
            for m in range(n_chunk):
                r = pl.ds(m * chunk, chunk)
                up[r] = dot(a_int[r], agg[l])
            if l == layers - 2:
                for m in range(n_chunk):
                    r = pl.ds(m * chunk, chunk)
                    mixt[l + 1, :, r] = mixed_last[r].T
            weight_term(l + 1, [pgs[pl.ds(m * chunk, chunk)] for m in range(n_chunk)])
            core_end(l + 1)
            rs_start(l + 1)
            t = 2 * layers - 2 - l
            arrived(t)
        for m in range(n_chunk):
            r = pl.ds(m * chunk, chunk)
            if l == layers - 1:
                above = cot[r].astype(F32)
            else:
                above = up[r] + dot(a_out[r], recv[t])
            pg = (above * dsilu[l, r]).astype(BF)
            pgs[r] = pg
            if l >= 1:
                mix = (1.0 - beta) * pg.astype(F32) + beta * dot_nt(pg, wts[l])
                agg[l - 1, r] = ((1.0 - RESTART) * mix).astype(BF)
    weight_term(0, [pgs[pl.ds(m * chunk, chunk)] for m in range(n_chunk)])

    down = tuple(reversed(range(layers)))
    core_end(0)
    rs_start(0)
    for l in down:
        rs_end(l)
        z_start(l)
    for l in down:
        z_end(l)
        ag_start(l)
    for l in down:
        ag_end(l)

    for t in range(table.shape[0]):
        drain(recv.at[t, pl.ds(0, n_nodes - cap)], tab_s.at[t])
    for l in down:
        drain(core_recv.at[l], core_s.at[l])
        drain(rs_recv.at[l, pl.ds(0, feat - share)], rs_s.at[l])
        drain(z_recv.at[l, pl.ds(0, (groups - 1) * share)], z_s.at[l])
        drain(wag.at[l, pl.ds(0, 2 * feat - share)], ag_s.at[l])


def store_kernel(hid, agg, wfull, hid_hbm, agg_hbm, wg_hbm, sem):
    copies = [
        pltpu.make_async_copy(src, dst, sem.at[i])
        for i, (src, dst) in enumerate(((hid, hid_hbm), (agg, agg_hbm), (wfull, wg_hbm)))
    ]
    for copy in copies:
        copy.start()
    for copy in copies:
        copy.wait()


def per_device(features, past_hidden, past_grads, cotangent, weights, inner_tiles, inner_blocks,
               outer_tiles, outer_blocks, slot_rows, slot_counts):
    owners = lax.axis_size("store")
    groups = lax.axis_size("group")
    nodes, feat = features.shape
    layers = weights.shape[0]
    blocks, per_row, tile, _ = inner_tiles.shape
    node_total = nodes * owners * groups
    share = feat // (owners // 2)
    anyspec = pl.BlockSpec(memory_space=pltpu.HBM)
    V = pltpu.VMEM
    S = pltpu.SemaphoreType.DMA
    res = pl.pallas_call(
        functools.partial(step_kernel, groups, owners, node_total),
        out_shape=(
            V((layers, nodes, feat), BF),
            V((layers - 1, nodes, feat), BF),
            V((layers, feat, feat), F32),
        ),
        in_specs=[anyspec] * 11,
        out_specs=(pl.BlockSpec(memory_space=V),) * 3,
        scratch_shapes=[
            V((5, nodes, feat), BF),
            V((nodes, feat), BF),
            V((layers, feat, feat), BF),
            V((blocks, per_row, tile, tile), BF),
            V((blocks, per_row, tile, tile), BF),
            pltpu.SMEM((per_row, blocks), jnp.int32),
            pltpu.SMEM((per_row, blocks), jnp.int32),
            pltpu.SMEM((1, owners), jnp.int32),
            V((1, nodes), jnp.int32),
            V((owners, tile), jnp.int32),
            V((nodes, nodes), BF),
            V((5, nodes, feat), BF),
            V((5, nodes, feat), BF),
            V((nodes, nodes), BF),
            V((nodes, nodes), BF),
            V((nodes, nodes), BF),
            V((layers, nodes, feat), F32),
            V((layers, feat, nodes), BF),
            V((nodes, feat), BF),
            V((nodes, feat), BF),
            V((nodes, feat), F32),
            V((layers, 2, feat, feat // 2), F32),
            V((layers, feat, feat // 2), F32),
            V((layers, feat, feat // 2), F32),
            V((layers, feat, feat // 2), F32),
            V((layers, share, feat // 2), F32),
            V((layers, groups * share, feat // 2), F32),
            V((layers, 2 * feat, feat // 2), BF),
            S((13,)), S, S, S((5,)), S((5,)),
            S((layers,)), S((layers,)), S((layers,)), S((layers,)),
            S((layers,)), S((layers,)), S((layers,)), S((layers,)),
        ],
        compiler_params=pltpu.CompilerParams(
            collective_id=0, has_side_effects=True, vmem_limit_bytes=60 << 20
        ),
        name="lmc_step",
    )(features, past_hidden, past_grads, cotangent, weights, inner_tiles, inner_blocks.T,
      outer_tiles, outer_blocks.T, slot_rows, slot_counts)
    return pl.pallas_call(
        store_kernel,
        out_shape=tuple(jax.ShapeDtypeStruct(r.shape, r.dtype) for r in res),
        in_specs=[pl.BlockSpec(memory_space=V)] * 3,
        out_specs=(anyspec,) * 3,
        scratch_shapes=[S((3,))],
        compiler_params=pltpu.CompilerParams(vmem_limit_bytes=1 << 20),
        name="store_results",
    )(*[pltpu.with_memory_space_constraint(r, V) for r in res])


def solution(mesh):
    placed = (
        P(("group", "store"), None),
        P(None, ("group", "store"), None),
        P(None, ("group", "store"), None),
        P(("group", "store"), None),
        P(),
        P(("group", "store"), None, None, None),
        P(("group", "store"), None),
        P(("group", "store"), None, None, None),
        P(("group", "store"), None),
        P(("group", "store"), None),
        P(("group", "store"), None),
    )
    return jax.shard_map(
        per_device,
        mesh=mesh,
        in_specs=placed,
        out_specs=(P(None, ("group", "store"), None), P(None, ("group", "store"), None), P()),
        check_vma=False,
    )
```

```python
import functools
import math

import jax
import jax.numpy as jnp
from jax import lax
from jax.experimental import pallas as pl
from jax.experimental.pallas import tpu as pltpu
from jax.sharding import PartitionSpec as P

RESTART = 0.1
MESH = pl.DeviceIdType.MESH
BF = jnp.bfloat16
F32 = jnp.float32


def beta_of(layer_idx):
    return math.log(0.5 / (layer_idx + 1) + 1.0)


def dot(lhs, rhs):
    return jnp.dot(lhs, rhs, preferred_element_type=F32)


def dot_nt(lhs, rhs):
    return lax.dot_general(lhs, rhs, (((1,), (1,)), ((), ())), preferred_element_type=F32)


def step_kernel(
    groups, owners, node_total,
    feat_hbm, past_h_hbm, past_g_hbm, cot_hbm, w_hbm, itile_hbm, iblk_hbm, otile_hbm, oblk_hbm,
    rows_hbm, cnt_hbm,
    hid, agg, wfull,
    table, cot, wts, itile, otile, iblk, oblk, cnt, rows, idx,
    onehot, sendbuf, recv, a_in, a_out, a_int, dsilu, mixt, mixed_last, pgs, up,
    wterm, core_recv, reduced, rs_recv, z_src, z_recv, wag,
    lsem, idx_s, idx_r, tab_s, tab_r, core_s, core_r, rs_s, rs_r, z_s, z_r, ag_s, ag_r,
):
    n_nodes, feat = table.shape[1], table.shape[2]
    layers = wts.shape[0]
    blocks, per_row, tile, _ = itile.shape
    cap = n_nodes // owners
    chips = owners // 2
    side = 4
    half = feat // 2
    share = feat // chips
    g = lax.axis_index("group")
    s = lax.axis_index("store")
    chip, core = s // 2, lax.rem(s, 2)
    cx, cy = chip // side, lax.rem(chip, side)

    def spread(j):
        return jnp.where(j == 0, 2, jnp.where(j == 1, 1, jnp.where(j == 2, 3, 0)))

    def chip_peer(j):
        return lax.rem(cx + spread(j // side), side) * side + lax.rem(cy + spread(lax.rem(j, side)), side)

    def peer(i):
        return chip_peer(i // 2) * 2 + lax.rem(core + 1 + lax.rem(i, 2), 2)

    def zpeer(i):
        mid = groups // 2
        return lax.rem(g + jnp.where(lax.rem(i, 2) == 0, mid + i // 2, mid - (i + 1) // 2), groups)

    ring = (2, 1, 3, 0)
    x_rows = [lax.rem(cx + a, side) for a in ring]
    steps = sorted(
        ((a, b, c) for a in range(side) for b in range(side) for c in range(2) if (a, b, c) != (0, 0, 0)),
        key=lambda p: (-min(p[0], side - p[0]) - min(p[1], side - p[1]), p[2], (p[0] + 2 * p[1]) % 4, p),
    )
    far = [
        (lax.rem(cx + a, side) * side + lax.rem(cy + b, side)) * 2 + lax.rem(core + c, 2) for a, b, c in steps
    ]
    far_chips = [
        lax.rem(cx + a, side) * side + lax.rem(cy + b, side) for a, b, c in steps if c == 0
    ]

    def each(count, act):
        def step(i, carry):
            act(i)
            return carry

        lax.fori_loop(0, count, step, 0)

    def block(index, size):
        return pl.ds(pl.multiple_of(index * size, size), size)

    def push(src, dst, send_sem, recv_sem, group, store):
        pltpu.make_async_remote_copy(
            src_ref=src, dst_ref=dst, send_sem=send_sem, recv_sem=recv_sem,
            device_id=(group, store), device_id_type=MESH,
        ).start()

    def drain(part, *sems):
        for sem in sems:
            pltpu.make_async_copy(part, part, sem).wait()

    loads = [
        pltpu.make_async_copy(src, dst, lsem.at[i])
        for i, (src, dst) in enumerate((
            (rows_hbm, rows),
            (cnt_hbm, cnt),
            (iblk_hbm, iblk),
            (oblk_hbm, oblk),
            (itile_hbm, itile),
            (otile_hbm, otile),
            (feat_hbm, table.at[0]),
            (past_h_hbm, table.at[pl.ds(1, 2)]),
            (past_g_hbm.at[1], table.at[3]),
            (past_g_hbm.at[0], table.at[4]),
            (w_hbm, wts),
            (cot_hbm, cot),
        ))
    ]
    loads[0].start()

    barrier = pltpu.get_barrier_semaphore()
    each(groups - 1, lambda i: pl.semaphore_signal(
        barrier, inc=1, device_id=(zpeer(i), s), device_id_type=MESH))
    for o in far:
        pl.semaphore_signal(barrier, inc=1, device_id=(g, o), device_id_type=MESH)
    for load in loads[1:]:
        load.start()
    loads[0].wait()
    pl.semaphore_wait(barrier, owners - 1 + groups - 1)

    def wanted_lanes(o):
        return rows.at[:, pl.ds(pl.multiple_of(o * cap // tile * tile, tile), tile)]

    for o in far:
        push(wanted_lanes(o), idx.at[pl.ds(s, 1)], idx_s, idx_r, g, o)

    own_idx = pltpu.make_async_copy(wanted_lanes(s), idx.at[pl.ds(s, 1)], lsem.at[12])
    own_idx.start()

    for load in loads[1:6]:
        load.wait()
    lane = lax.broadcasted_iota(jnp.int32, (1, tile), 1)
    per_chunk = tile // cap

    def build(b):
        in_tiles = [itile[b, k] for k in range(per_row)]
        in_tiles_t = [t.T for t in in_tiles]
        out_tiles = [otile[b, k] for k in range(per_row)]
        for c in range(blocks):
            live_to = jnp.zeros((1, tile), jnp.int32)
            for q in range(per_chunk):
                live_to = jnp.where(lane // cap == q, cnt[0, c * per_chunk + q], live_to)
            live = (lane % cap < live_to).astype(F32)
            din = jnp.zeros((tile, tile), BF)
            dint = jnp.zeros((tile, tile), BF)
            dout = jnp.zeros((tile, tile), BF)
            for k in range(per_row):
                keep = (jnp.full((1, tile), iblk[k, b], jnp.int32) == c).astype(F32).astype(BF)
                din = din + in_tiles[k] * keep
                dint = dint + in_tiles_t[k] * keep
                keep = (live * (jnp.full((1, tile), oblk[k, b], jnp.int32) == c).astype(F32)).astype(BF)
                dout = dout + out_tiles[k] * keep
            here = block(b, tile)
            a_in[here, pl.ds(c * tile, tile)] = din
            a_out[here, pl.ds(c * tile, tile)] = dout
            a_int[pl.ds(c * tile, tile), here] = dint

    each(blocks, build)
    own_idx.wait()
    for load in loads[6:]:
        load.wait()
    drain(idx.at[pl.ds(0, owners - 1)], idx_r, idx_s)

    chunk = n_nodes // side
    n_chunk = side
    per_quarter = owners // side

    ranked = far + [s]

    def make_onehot(quarter):
        asked = [idx[pl.ds(o, 1)] for o in ranked[quarter * per_quarter:(quarter + 1) * per_quarter]]
        part = jnp.concatenate(asked, axis=0).astype(F32)
        wide = jnp.broadcast_to(part[:, None, :], (per_quarter, cap, tile)).reshape(chunk, tile)
        place = lax.broadcasted_iota(jnp.int32, (chunk, tile), 0) % cap + lax.rem(s, per_chunk) * cap
        at = lax.broadcasted_iota(jnp.int32, (chunk, tile), 1)
        col = jnp.sum(jnp.where(place == at, wide, 0.0), axis=1, keepdims=True)
        node = lax.broadcasted_iota(jnp.int32, (chunk, n_nodes), 1).astype(F32)
        hot = jnp.where(node == col, 1.0, 0.0).astype(BF)
        onehot[pl.ds(quarter * chunk, chunk)] = hot
        return hot

    def pull(t, hot_of):
        for quarter in range(side):
            first = quarter * per_quarter
            sendbuf[t, pl.ds(quarter * chunk, chunk)] = dot(hot_of(quarter), table[t]).astype(BF)
            for i in range(first, first + per_quarter):
                if i < owners - 1:
                    push(sendbuf.at[t, pl.ds(i * cap, cap)], recv.at[t, block(s, cap)],
                         tab_s.at[t], tab_r.at[t], g, ranked[i])
        recv[t, block(s, cap)] = sendbuf[t, pl.ds((owners - 1) * cap, cap)]

    pull(0, make_onehot)
    each(table.shape[0] - 1, lambda t: pull(t + 1, lambda quarter: onehot[pl.ds(quarter * chunk, chunk)]))

    def arrived(t):
        drain(recv.at[t, pl.ds(0, n_nodes - cap)], tab_r.at[t])

    for l in range(layers):
        beta = beta_of(l)
        arrived(l)

        def forward(m, l=l, beta=beta):
            r = pl.ds(m * chunk, chunk)
            h_now = table[0] if l == 0 else hid[l - 1]
            total = dot(a_in[r], h_now) + dot(a_out[r], recv[l])
            mixed = ((1.0 - RESTART) * total + RESTART * table[0, r].astype(F32)).astype(BF)
            pre = (1.0 - beta) * mixed.astype(F32) + beta * dot(mixed, wts[l])
            q = jax.nn.sigmoid(pre)
            act = pre * q
            hid[l, r] = act.astype(BF)
            dsilu[l, r] = q + act * (1.0 - q)
            if l < layers - 1:
                mixt[l, :, r] = mixed.T
            else:
                mixed_last[r] = mixed

        for m in range(n_chunk):
            forward(m)

    def core_start(l):
        push(wterm.at[l, 1 - core], core_recv.at[l], core_s.at[l], core_r.at[l], g, chip * 2 + 1 - core)

    def core_end(l):
        drain(core_recv.at[l], core_r.at[l])
        reduced[l] = wterm[l, core] + core_recv[l]

    def rs_start(l):
        def go(k):
            push(reduced.at[l, block(k, share)], rs_recv.at[l, block(chip, share)],
                 rs_s.at[l], rs_r.at[l], g, k * 2 + core)

        if l <= 1:
            for k in far_chips:
                go(k)
        else:
            each(chips - 1, lambda j: go(chip_peer(j)))
        rs_recv[l, block(chip, share)] = reduced[l, block(chip, share)]

    def rs_end(l):
        drain(rs_recv.at[l, pl.ds(0, feat - share)], rs_r.at[l])
        z_src[l] = jnp.sum(rs_recv[l].reshape(chips, share, half), axis=0)

    def z_start(l):
        each(groups - 1, lambda i: push(
            z_src.at[l], z_recv.at[l, block(g, share)], z_s.at[l], z_r.at[l], zpeer(i), s))
        z_recv[l, block(g, share)] = z_src[l]

    def z_end(l):
        drain(z_recv.at[l, pl.ds(0, (groups - 1) * share)], z_r.at[l])
        total = jnp.sum(z_recv[l].reshape(groups, share, half), axis=0)
        wag[l, block(core * chips + chip, share)] = (
            total * (beta_of(l) / math.sqrt(node_total))).astype(BF)

    def ag_start(l):
        own = block(core * chips + chip, share)

        def go(o):
            push(wag.at[l, own], wag.at[l, own], ag_s.at[l], ag_r.at[l], g, o)

        if l == 0:
            for o in far:
                go(o)
        else:
            each(owners - 1, lambda i: go(peer(i)))

    def ag_end(l):
        drain(wag.at[l, pl.ds(0, 2 * feat - share)], ag_r.at[l])
        for c in range(2):
            wfull[l, :, c * half:(c + 1) * half] = wag[l, c * feat:(c + 1) * feat].astype(F32)

    def weight_term(l, pgs):
        wsum = [None, None]
        for m, pg in enumerate(pgs):
            r = pl.ds(m * chunk, chunk)
            part = dot(mixt[l, :, r], pg)
            for c in range(2):
                cols = part[:, c * half:(c + 1) * half]
                wsum[c] = cols if m == 0 else wsum[c] + cols
        for c in range(2):
            wterm[l, c] = wsum[c]
        core_start(l)

    for l in reversed(range(layers)):
        beta = beta_of(l)
        if l < layers - 1:
            for m in range(n_chunk):
                r = pl.ds(m * chunk, chunk)
                up[r] = dot(a_int[r], agg[l])
            if l == layers - 2:
                for m in range(n_chunk):
                    r = pl.ds(m * chunk, chunk)
                    mixt[l + 1, :, r] = mixed_last[r].T
            weight_term(l + 1, [pgs[pl.ds(m * chunk, chunk)] for m in range(n_chunk)])
            if l >= 1:
                core_end(l + 1)
                rs_start(l + 1)
            t = 2 * layers - 2 - l
            arrived(t)
        for m in range(n_chunk):
            r = pl.ds(m * chunk, chunk)
            if l == layers - 1:
                above = cot[r].astype(F32)
            else:
                above = up[r] + dot(a_out[r], recv[t])
            pg = (above * dsilu[l, r]).astype(BF)
            pgs[r] = pg
            if l >= 1:
                mix = (1.0 - beta) * pg.astype(F32) + beta * dot_nt(pg, wts[l])
                agg[l - 1, r] = ((1.0 - RESTART) * mix).astype(BF)
    weight_term(0, [pgs[pl.ds(m * chunk, chunk)] for m in range(n_chunk)])

    down = tuple(reversed(range(layers)))
    core_end(1)
    rs_start(1)
    core_end(0)
    rs_start(0)
    for l in down:
        rs_end(l)
        z_start(l)
    for l in down:
        z_end(l)
        ag_start(l)
    for t in range(table.shape[0]):
        drain(recv.at[t, pl.ds(0, n_nodes - cap)], tab_s.at[t])
    for l in down:
        drain(core_recv.at[l], core_s.at[l])
        drain(rs_recv.at[l, pl.ds(0, feat - share)], rs_s.at[l])
        drain(z_recv.at[l, pl.ds(0, (groups - 1) * share)], z_s.at[l])
    for l in down:
        drain(wag.at[l, pl.ds(0, 2 * feat - share)], ag_s.at[l])
        ag_end(l)


def store_kernel(hid, agg, wfull, hid_hbm, agg_hbm, wg_hbm, sem):
    copies = [
        pltpu.make_async_copy(src, dst, sem.at[i])
        for i, (src, dst) in enumerate(((hid, hid_hbm), (agg, agg_hbm), (wfull, wg_hbm)))
    ]
    for copy in copies:
        copy.start()
    for copy in copies:
        copy.wait()


def per_device(features, past_hidden, past_grads, cotangent, weights, inner_tiles, inner_blocks,
               outer_tiles, outer_blocks, slot_rows, slot_counts):
    owners = lax.axis_size("store")
    groups = lax.axis_size("group")
    nodes, feat = features.shape
    layers = weights.shape[0]
    blocks, per_row, tile, _ = inner_tiles.shape
    node_total = nodes * owners * groups
    share = feat // (owners // 2)
    anyspec = pl.BlockSpec(memory_space=pltpu.HBM)
    V = pltpu.VMEM
    S = pltpu.SemaphoreType.DMA
    res = pl.pallas_call(
        functools.partial(step_kernel, groups, owners, node_total),
        out_shape=(
            V((layers, nodes, feat), BF),
            V((layers - 1, nodes, feat), BF),
            V((layers, feat, feat), F32),
        ),
        in_specs=[anyspec] * 11,
        out_specs=(pl.BlockSpec(memory_space=V),) * 3,
        scratch_shapes=[
            V((5, nodes, feat), BF),
            V((nodes, feat), BF),
            V((layers, feat, feat), BF),
            V((blocks, per_row, tile, tile), BF),
            V((blocks, per_row, tile, tile), BF),
            pltpu.SMEM((per_row, blocks), jnp.int32),
            pltpu.SMEM((per_row, blocks), jnp.int32),
            pltpu.SMEM((1, owners), jnp.int32),
            V((1, nodes), jnp.int32),
            V((owners, tile), jnp.int32),
            V((nodes, nodes), BF),
            V((5, nodes, feat), BF),
            V((5, nodes, feat), BF),
            V((nodes, nodes), BF),
            V((nodes, nodes), BF),
            V((nodes, nodes), BF),
            V((layers, nodes, feat), F32),
            V((layers, feat, nodes), BF),
            V((nodes, feat), BF),
            V((nodes, feat), BF),
            V((nodes, feat), F32),
            V((layers, 2, feat, feat // 2), F32),
            V((layers, feat, feat // 2), F32),
            V((layers, feat, feat // 2), F32),
            V((layers, feat, feat // 2), F32),
            V((layers, share, feat // 2), F32),
            V((layers, groups * share, feat // 2), F32),
            V((layers, 2 * feat, feat // 2), BF),
            S((13,)), S, S, S((5,)), S((5,)),
            S((layers,)), S((layers,)), S((layers,)), S((layers,)),
            S((layers,)), S((layers,)), S((layers,)), S((layers,)),
        ],
        compiler_params=pltpu.CompilerParams(
            collective_id=0, has_side_effects=True, vmem_limit_bytes=60 << 20
        ),
        name="lmc_step",
    )(features, past_hidden, past_grads, cotangent, weights, inner_tiles, inner_blocks.T,
      outer_tiles, outer_blocks.T, slot_rows, slot_counts)
    return pl.pallas_call(
        store_kernel,
        out_shape=tuple(jax.ShapeDtypeStruct(r.shape, r.dtype) for r in res),
        in_specs=[pl.BlockSpec(memory_space=V)] * 3,
        out_specs=(anyspec,) * 3,
        scratch_shapes=[S((3,))],
        compiler_params=pltpu.CompilerParams(vmem_limit_bytes=1 << 20),
        name="store_results",
    )(*[pltpu.with_memory_space_constraint(r, V) for r in res])


def solution(mesh):
    placed = (
        P(("group", "store"), None),
        P(None, ("group", "store"), None),
        P(None, ("group", "store"), None),
        P(("group", "store"), None),
        P(),
        P(("group", "store"), None, None, None),
        P(("group", "store"), None),
        P(("group", "store"), None, None, None),
        P(("group", "store"), None),
        P(("group", "store"), None),
        P(("group", "store"), None),
    )
    return jax.shard_map(
        per_device,
        mesh=mesh,
        in_specs=placed,
        out_specs=(P(None, ("group", "store"), None), P(None, ("group", "store"), None), P()),
        check_vma=False,
    )
```
